128 devices in a mesh: row: 8 (over z, core), col: 8 (over x_lo, y), depth: 2 (over x_hi).
Axes of the slice: x: 4 (x_hi: 2, x_lo: 2; x = x_hi * 2 + x_lo), y: 4, z: 4, core: 2. Of those that a mesh axis runs over, the one named last changes fastest.
Arguments:
- blocks: bfloat16 [256, 16, 4096], P('row', ('col', 'depth')), may hold values from -1 to 1
- pattern: int32 [256, 16], P('row', ('col', 'depth')), may hold values from 0 to 255, as said below
Outputs:
- purified: float32 [2048, 16384], P('row', ('col', 'depth'))
The draws below stay inside these ranges and needn't reach their ends.
Inputs may be any that keep to these rules, and one draw needn't show every extreme that they name: `pattern`: in every block row, entries j * 1 to j + 1 - 1 name 1 different block columns of j * 16 to j * 16 + 15, in increasing order.
All inputs are finite; a program needn't handle non-finite values.
Results may differ from the reference program's by a relative error of at most 0.0028.
Values may be sent and summed in bfloat16 or wider, within the bound.
No kernel may reach another device: no remote copies, remote signals or barrier semaphores. Data moves between devices by JAX's collectives and lax.ppermute only.
A program may use at most 256 MiB of HBM per device.

```python
import jax
import jax.numpy as jnp
from jax import lax

BLOCK = 64
NBP = 32
KB = 1
SR = 4
NB = 256
NBC = 16
KSLOTS = 16
SLAB = 32
N_ROW = 8


def draw_pattern(key, part):
    groups = KSLOTS // KB
    scores = jax.random.randint(key, (NB, groups, NBC), 0, 1 << 20)
    scores = scores.at[0, 0, 0].set(-1)
    scores = scores.at[0, groups - 1, NBC - 1].set(-1)
    keyed = scores * NBC + jnp.arange(NBC, dtype=jnp.int32)[None, None, :]
    chosen = jnp.argsort(keyed, axis=-1)[..., :KB]
    chosen = jnp.sort(chosen, axis=-1)
    placed = chosen + (jnp.arange(groups, dtype=jnp.int32) * NBC)[None, :, None]
    return placed.reshape(NB, KSLOTS).astype(jnp.int32)


def steps_of(rng, extent, pieces, low, top_value):
    factor_of, own = 1.0, jax.random.fold_in(rng, 6)
    for axis_at, shards_of in pieces:
        heights = jnp.exp(jax.random.uniform(jax.random.fold_in(own, axis_at), (shards_of,), jnp.float32, low / len(pieces), top_value / len(pieces)))
        factor_of = factor_of * jnp.repeat(heights, extent[axis_at] // shards_of).reshape([-1 if axis == axis_at else 1 for axis in range(len(extent))])
    return factor_of


def normal_values(own_key, extent, scale, limit, pieces=(), kind=jnp.bfloat16):
    gain = steps_of(own_key, extent, pieces, -0.22, 0.18) if pieces else 1.0
    drawn = jax.random.normal(own_key, extent, jnp.float32) * scale * gain
    return jnp.minimum(jnp.maximum(drawn, -limit), limit).astype(kind)


def setup_inputs(seed: int = 0) -> dict:
    splits = jax.random.split(jax.random.key(seed), 3)
    return {
        "blocks": normal_values(splits[0], (NB, KSLOTS, BLOCK * BLOCK), 40 ** -0.5, 1.0, ((0, 8), (1, 16))),
        "pattern": draw_pattern(jax.random.fold_in(splits[2], 71), 0),
    }


def reference(blocks, pattern):
    tiles = blocks.reshape(NB, KSLOTS, BLOCK, BLOCK)
    slab_index = (jnp.arange(N_ROW, dtype=jnp.int32)[:, None] * NBP + jnp.arange(SR, dtype=jnp.int32)[None, :]).reshape(-1)

    def dense_row(index):
        grid = jnp.zeros((NB, BLOCK, BLOCK), jnp.float32)
        return grid.at[pattern[index]].set(tiles[index].astype(jnp.float32))

    def square_row(index):
        stacked = jax.vmap(dense_row)(pattern[index])
        result = jnp.einsum("syz,skzc->ykc", tiles[index].astype(jnp.float32), stacked)
        return result.reshape(BLOCK, NB * BLOCK)

    square32 = lax.map(square_row, slab_index).reshape(SLAB * BLOCK, NB * BLOCK)
    square = square32.astype(jnp.bfloat16)

    def add_row(index, total):
        start = jnp.asarray(index).astype(jnp.int32) * BLOCK
        columns = lax.dynamic_slice_in_dim(square, start, BLOCK, 1).astype(jnp.float32)
        terms = jnp.einsum("ry,syz->rsz", columns, tiles[index].astype(jnp.float32))
        return total.at[:, pattern[index], :].add(terms)

    cube_sum = lax.fori_loop(0, NB, add_row, jnp.zeros((SLAB * BLOCK, NB, BLOCK), jnp.float32))
    cube_sum = cube_sum.reshape(SLAB * BLOCK, NB * BLOCK)
    return 3.0 * square32 - 2.0 * cube_sum
```

```python
import functools

import jax
import jax.numpy as jnp
from jax import lax
from jax.experimental import pallas as pl
from jax.experimental.pallas import tpu as pltpu
from jax.sharding import PartitionSpec as P

AXES = ("row", "col", "depth")
F32, BF16, I32 = jnp.float32, jnp.bfloat16, jnp.int32
PACKED = 1040
SLABP = 144
VMEM_LIMIT = 40 << 20
PARAMS = pltpu.CompilerParams(vmem_limit_bytes=VMEM_LIMIT)


def place(i):
    row, col, depth = i // 16, i // 2 % 8, i % 2
    return row // 2, row % 2, depth * 2 + col // 4, col % 4


def index(z, core, x, y):
    return (z * 2 + core) * 16 + (x % 2 * 4 + y) * 2 + x // 2


def permute(value, target):
    pairs = [(i, index(*target(*place(i)))) for i in range(128)]
    return lax.ppermute(value, AXES, pairs)


def shift(value, z=0, core=0, x=0, y=0):
    return permute(
        value, lambda a, b, c, d: ((a + z) % 4, (b + core) % 2, (c + x) % 4, (d + y) % 4)
    )


def swap_rows_and_y(value):
    def target(z, core, x, y):
        t = z % 2 * 2 + core
        return z // 2 * 2 + y // 2, y % 2, x, t

    return permute(value, target)


def over_row(value):
    ring = [value] + [shift(value, z=d) for d in (1, 3, 2)]
    return ring + [shift(v, core=1) for v in ring]


def pack_kernel(x_ref, pat_ref, packed_ref, slab_ref, rows, nat, turned, ints):
    for e in range(32):
        rows[pl.ds(e, 32, stride=32), :] = x_ref[:, e * 128 : e * 128 + 128].astype(F32)
    for quad in range(8):
        at = pl.ds(quad * 128, 128)
        packed_ref[at, :] = jnp.transpose(rows[at, :]).astype(BF16)
    ints[...] = jnp.zeros_like(ints)
    ints[0:1, 0:32] = pat_ref[...]
    columns = ints[...].astype(F32).astype(BF16)
    packed_ref[1024:1040, :] = columns
    for i in range(4):
        part = rows[i * 32 : i * 32 + 32, :]
        nat[pl.ds(i * 64, 32, stride=2), :] = part
        nat[pl.ds(i * 64 + 1, 32, stride=2), :] = pltpu.roll(part, 64, 1)
    for h in range(2):
        turned[...] = jnp.transpose(nat[h * 128 : h * 128 + 128, :])
        for p in range(2):
            piece = turned[pl.ds(p, 32, stride=2), :].astype(BF16)
            at = h * 64 + p * 32
            for s in range(16):
                slab_ref[s, at : at + 32, :] = piece
    for s in range(16):
        slab_ref[s, 128:144, :] = columns


def pack(blocks, pattern):
    return pl.pallas_call(
        pack_kernel,
        out_shape=(
            jax.ShapeDtypeStruct((PACKED, 128), BF16),
            jax.ShapeDtypeStruct((16, SLABP, 128), BF16),
        ),
        scratch_shapes=[
            pltpu.VMEM((1024, 128), F32),
            pltpu.VMEM((256, 128), F32),
            pltpu.VMEM((128, 128), F32),
            pltpu.VMEM((16, 128), I32),
        ],
        compiler_params=PARAMS,
        name="pack",
    )(blocks, pattern)


def fetch_rows(place_ref, parts, panel, sem):
    z, core = place_ref[0], place_ref[1]
    copies = []
    for n, part in enumerate(parts):
        source_z = lax.rem(z + 4 - (0, 1, 3, 2)[n % 4], 4)
        source_core = core if n < 4 else 1 - core
        copies.append(
            pltpu.make_async_copy(part, panel.at[source_z * 2 + source_core], sem.at[n])
        )
    for copy in copies:
        copy.start()
    return copies


def lane_masks():
    lane = lax.broadcasted_iota(I32, (1, 256), 1)
    return lax.rem(lax.div(lane, 32), 4)


def square_kernel(place_ref, *refs):
    parts, (slab, out32, out16, panel, ints, scal, sem, sem_s) = refs[:8], refs[8:]
    copies = fetch_rows(place_ref, parts, panel, sem)
    out32[...] = jnp.zeros_like(out32)
    for s in range(16):
        ints[8 + s : 9 + s, :] = slab[s, 128:144, :].astype(F32)[0:1, :].astype(I32)
    for copy in copies:
        copy.wait()
    for r in range(8):
        ints[r : r + 1, :] = panel[r, 1024:1040, :].astype(F32)[0:1, :].astype(I32)
    to_scal = pltpu.make_async_copy(ints, scal, sem_s)
    to_scal.start()
    to_scal.wait()
    quarter = lane_masks()
    half = lax.broadcasted_iota(I32, (64, 128), 1) < 64

    def step(s, carry):
        sides = []
        for h in range(2):
            pieces = []
            for p in range(2):
                pieces += [slab[s, h * 64 + p * 32 : h * 64 + p * 32 + 32, :]] * 4
            sides.append(jnp.concatenate(pieces, axis=0))
        rhs = jnp.concatenate(sides, axis=1)
        left, columns = [], []
        for i in range(4):
            c = scal[8 + s, i]
            r, k = lax.div(c, 32), lax.rem(c, 32)
            quad, c4 = lax.div(k, 4), lax.rem(k, 4)
            t = panel[r, pl.ds(pl.multiple_of(quad * 128, 128), 128), :]
            t = jnp.concatenate([t[0:64], t[64:128]], axis=1)
            left.append(t * (quarter == c4).astype(F32).astype(BF16))
            columns.append(lax.rem(scal[r, k], 16))
        out = jnp.dot(jnp.concatenate(left, axis=0), rhs, preferred_element_type=F32)
        for i in range(4):
            h = i // 2
            got = out[i * 64 : i * 64 + 64, h * 128 : h * 128 + 128]
            got = jnp.where(half if i % 2 == 0 else jnp.logical_not(half), got, 0.0)
            out32[h, pl.ds(pl.multiple_of(columns[i] * 64, 64), 64), :] += got
        return carry

    lax.fori_loop(0, 16, step, 0)
    for h in range(2):
        for quad in range(4):
            for p in range(2):
                for c4 in range(4):
                    take = out32[h, pl.ds((quad * 4 + c4) * 64 + p, 32, stride=2), :]
                    at = quad * 256 + p * 128 + c4 * 32
                    out16[h, at : at + 32, :] = take.astype(BF16)


ANY = pl.BlockSpec(memory_space=pl.ANY)
SMEM = pl.BlockSpec(memory_space=pltpu.SMEM)
VMEM = pl.BlockSpec(memory_space=pltpu.VMEM)


def square_of(where, parts, slab):
    return pl.pallas_call(
        square_kernel,
        out_shape=(
            jax.ShapeDtypeStruct((2, 1024, 128), F32),
            jax.ShapeDtypeStruct((2, 1024, 128), BF16),
        ),
        in_specs=[SMEM] + [ANY] * 8 + [VMEM],
        out_specs=(VMEM, VMEM),
        scratch_shapes=[
            pltpu.VMEM((8, PACKED, 128), BF16),
            pltpu.VMEM((24, 128), I32),
            pltpu.SMEM((24, 128), I32),
            pltpu.SemaphoreType.DMA((8,)),
            pltpu.SemaphoreType.DMA,
        ],
        compiler_params=PARAMS,
        name="square",
    )(where, *parts, slab)


def cube_kernel(place_ref, *refs):
    parts, squares = refs[:8], refs[8:12]
    own, out1, out3, out2, panel, sq, acc, ints, scal, sem, sem_q, sem_s = refs[12:]
    x, y = place_ref[2], place_ref[3]
    copies = fetch_rows(place_ref, parts, panel, sem)
    more = []
    for n, part in enumerate(squares):
        source = lax.rem(x + 4 - (0, 1, 3, 2)[n], 4)
        more.append(pltpu.make_async_copy(part, sq.at[source], sem_q.at[n]))
    for copy in more:
        copy.start()
    acc[...] = jnp.zeros_like(acc)
    for copy in copies:
        copy.wait()
    for r in range(8):
        ints[r : r + 1, :] = panel[r, 1024:1040, :].astype(F32)[0:1, :].astype(I32)
    to_scal = pltpu.make_async_copy(ints, scal, sem_s)
    to_scal.start()
    to_scal.wait()
    for copy in more:
        copy.wait()
    quarter = lane_masks()
    masks = [(quarter == n).astype(F32).astype(BF16) for n in range(4)]

    def step(n, carry):
        q, hi, quad = lax.div(n, 8), lax.rem(lax.div(n, 4), 2), lax.rem(n, 4)
        at = pl.ds(pl.multiple_of(quad * 256, 256), 256)
        right = jnp.concatenate([sq[q + 2 * hi, h, at, :] for h in range(2)], axis=1)
        rows = pl.ds(pl.multiple_of((hi * 4 + quad) * 128, 128), 128)
        for there in range(4):
            t = panel[4 * q + there, rows, :]
            t = jnp.concatenate([t[0:64], t[64:128]], axis=1)
            left = jnp.concatenate([t * mask for mask in masks], axis=0)
            out = jnp.dot(left, right, preferred_element_type=F32)
            for c4 in range(4):
                j = lax.rem(scal[4 * q + there, hi * 16 + quad * 4 + c4], 16)
                into = pl.ds(pl.multiple_of(j * 64, 64), 64)
                acc[there, into, :] += out[c4 * 64 : c4 * 64 + 64, :]
        return carry

    lax.fori_loop(0, 16, step, 0)
    own[...] = acc[y]
    for d, ref in ((1, out1), (3, out3), (2, out2)):
        ref[...] = acc[lax.rem(y + d, 4)].astype(BF16)


def cube_of(where, parts, squares):
    return pl.pallas_call(
        cube_kernel,
        out_shape=(
            jax.ShapeDtypeStruct((1024, 256), F32),
            *[jax.ShapeDtypeStruct((1024, 256), BF16)] * 3,
        ),
        in_specs=[SMEM] + [ANY] * 12,
        out_specs=(VMEM,) * 4,
        scratch_shapes=[
            pltpu.VMEM((8, PACKED, 128), BF16),
            pltpu.VMEM((4, 2, 1024, 128), BF16),
            pltpu.VMEM((4, 1024, 256), F32),
            pltpu.VMEM((8, 128), I32),
            pltpu.SMEM((8, 128), I32),
            pltpu.SemaphoreType.DMA((8,)),
            pltpu.SemaphoreType.DMA((4,)),
            pltpu.SemaphoreType.DMA,
        ],
        compiler_params=PARAMS,
        name="cube",
    )(where, *parts, *squares)


def finish_kernel(sq_ref, own_ref, a_ref, b_ref, c_ref, out_ref):
    for m in range(8):
        at = pl.ds(m * 128, 128)
        for h in range(2):
            lanes = pl.ds(h * 128, 128)
            cube = own_ref[at, lanes]
            for ref in (a_ref, b_ref, c_ref):
                cube += ref[at, lanes].astype(F32)
            total = 3.0 * sq_ref[h, at, :] - 2.0 * cube
            out_ref[lanes, at] = jnp.transpose(total)


def finish(square32, own, others):
    return pl.pallas_call(
        finish_kernel,
        out_shape=jax.ShapeDtypeStruct((256, 1024), F32),
        in_specs=[VMEM] * 5,
        out_specs=VMEM,
        compiler_params=PARAMS,
        name="finish",
    )(square32, own, *others)


def body(blocks, pattern):
    row, col, depth = (lax.axis_index(a) for a in AXES)
    where = jnp.stack([row // 2, row % 2, depth * 2 + col // 4, col % 4]).astype(I32)
    packed, slab = pack(blocks.reshape(32, 4096), pattern.reshape(1, 32))
    parts = over_row(packed)
    slab = lax.all_to_all(slab, ("col", "depth"), 0, 0, tiled=True)
    turned = over_row(swap_rows_and_y(packed))
    square32, square16 = square_of(where, parts, slab)
    squares = [square16] + [shift(square16, x=d) for d in (1, 3, 2)]
    own, out1, out3, out2 = cube_of(where, turned, squares)
    others = [shift(out1, y=1), shift(out3, y=3), shift(out2, y=2)]
    return finish(square32, own, others)


def solution(mesh):
    in_specs = (P("row", ("col", "depth"), None), P("row", ("col", "depth")))
    out_specs = P("row", ("col", "depth"))
    return jax.shard_map(body, mesh=mesh, in_specs=in_specs, out_specs=out_specs, check_vma=False)
```

```python
import functools

import jax
import jax.numpy as jnp
from jax import lax
from jax.experimental import pallas as pl
from jax.experimental.pallas import tpu as pltpu
from jax.sharding import PartitionSpec as P

AXES = ("row", "col", "depth")
F32, BF16, I32 = jnp.float32, jnp.bfloat16, jnp.int32
HALF = 528
SLABP = 144
VMEM_LIMIT = 40 << 20
PARAMS = pltpu.CompilerParams(vmem_limit_bytes=VMEM_LIMIT)


def place(i):
    row, col, depth = i // 16, i // 2 % 8, i % 2
    return row // 2, row % 2, depth * 2 + col // 4, col % 4


def index(z, core, x, y):
    return (z * 2 + core) * 16 + (x % 2 * 4 + y) * 2 + x // 2


def permute(value, target):
    pairs = [(i, index(*target(*place(i)))) for i in range(128)]
    return lax.ppermute(value, AXES, pairs)


def swap(value, z=0, core=0, x=0, y=0):
    return permute(value, lambda a, b, c, d: (a ^ z, b ^ core, c ^ x, d ^ y))


def after(value, *first):
    return lax.optimization_barrier((value, *first))[0]


def rows_to_y(value):
    def target(z, core, x, y):
        t = z % 2 * 2 + core
        return z // 2 * 2 + y // 2, y % 2, x, t

    return permute(value, target)


FLIPS = (0, 1, 3, 2)


def ring_parts(value):
    return [value] + [swap(value, z=d) for d in FLIPS[1:]]


def fetch_rows(place_ref, ring, other, panel, sem):
    z, core = place_ref[0], place_ref[1]
    copies = []
    for n in range(4):
        row = (z ^ FLIPS[n]) * 2
        mine, others = panel.at[pl.ds((row + core) * 2, 2)], panel.at[pl.ds((row + 1 - core) * 2, 2)]
        copies.append(pltpu.make_async_copy(ring[n], mine, sem.at[n]))
        copies.append(pltpu.make_async_copy(other[n], others, sem.at[4 + n]))
    for copy in copies:
        copy.start()
    return copies


def pack_kernel(x_hbm, pat_hbm, packed_ref, slab_ref, x_ref, pat_ref, rows, nat, turned, ints, sem):
    copies = [
        pltpu.make_async_copy(x_hbm, x_ref, sem.at[0]),
        pltpu.make_async_copy(pat_hbm, pat_ref, sem.at[1]),
    ]
    for copy in copies:
        copy.start()
    for copy in copies:
        copy.wait()
    for e in range(32):
        rows[pl.ds(e, 32, stride=32), :] = x_ref[:, e * 128 : e * 128 + 128].astype(F32)
    ints[...] = jnp.zeros_like(ints)
    for half in range(2):
        for quad in range(4):
            at = pl.ds(half * 512 + quad * 128, 128)
            packed_ref[half, quad * 128 : quad * 128 + 128, :] = jnp.transpose(rows[at, :]).astype(BF16)
        ints[0:1, 0:16] = pat_ref[0:1, half * 16 : half * 16 + 16]
        packed_ref[half, 512:528, :] = ints[...].astype(F32).astype(BF16)
    columns = packed_ref[0, 512:528, :]
    for i in range(4):
        part = rows[i * 32 : i * 32 + 32, :]
        nat[pl.ds(i * 64, 32, stride=2), :] = part
        nat[pl.ds(i * 64 + 1, 32, stride=2), :] = pltpu.roll(part, 64, 1)
    for h in range(2):
        turned[...] = jnp.transpose(nat[h * 128 : h * 128 + 128, :])
        for p in range(2):
            piece = turned[pl.ds(p, 32, stride=2), :].astype(BF16)
            at = h * 64 + p * 32
            for s in range(16):
                slab_ref[s, at : at + 32, :] = piece
    for s in range(16):
        slab_ref[s, 128:144, :] = columns


ANY = pl.BlockSpec(memory_space=pl.ANY)
HBM = pl.BlockSpec(memory_space=pltpu.HBM)
SMEM = pl.BlockSpec(memory_space=pltpu.SMEM)
VMEM = pl.BlockSpec(memory_space=pltpu.VMEM)


def pack(blocks, pattern):
    return pl.pallas_call(
        pack_kernel,
        out_shape=(
            jax.ShapeDtypeStruct((2, HALF, 128), BF16),
            jax.ShapeDtypeStruct((16, SLABP, 128), BF16),
        ),
        in_specs=[HBM, HBM],
        out_specs=(VMEM, VMEM),
        scratch_shapes=[
            pltpu.VMEM((32, 4096), BF16),
            pltpu.VMEM((1, 32), I32),
            pltpu.VMEM((1024, 128), F32),
            pltpu.VMEM((256, 128), F32),
            pltpu.VMEM((128, 128), F32),
            pltpu.VMEM((16, 128), I32),
            pltpu.SemaphoreType.DMA((2,)),
        ],
        compiler_params=pltpu.CompilerParams(vmem_limit_bytes=62 << 20),
        name="pack",
    )(blocks, pattern)


def read_columns(panel, ints):
    for n in range(16):
        row = panel[n, 512:528, :].astype(F32)[0:1, :]
        ints[n : n + 1, :] = row.astype(I32)


def lane_masks():
    lane = lax.broadcasted_iota(I32, (1, 256), 1)
    return lax.rem(lax.div(lane, 32), 4)


def square_kernel(place_ref, *refs):
    ring, other, slab_ref = refs[:4], refs[4:8], refs[8]
    out32, out_a, out_b, panel, slab, ints, scal, sem = refs[9:]
    copies = fetch_rows(place_ref, ring, other, panel, sem)
    fetch_slab = pltpu.make_async_copy(slab_ref, slab, sem.at[8])
    fetch_slab.start()
    out32[...] = jnp.zeros_like(out32)
    fetch_slab.wait()
    for s in range(16):
        ints[16 + s : 17 + s, :] = slab[s, 128:144, :].astype(F32)[0:1, :].astype(I32)
    for copy in copies:
        copy.wait()
    read_columns(panel, ints)
    to_scal = pltpu.make_async_copy(ints, scal, sem.at[0])
    to_scal.start()
    to_scal.wait()
    quarter = lane_masks()
    half = lax.broadcasted_iota(I32, (64, 128), 1) < 64

    def step(s, carry):
        sides = []
        for h in range(2):
            pieces = []
            for p in range(2):
                pieces += [slab[s, h * 64 + p * 32 : h * 64 + p * 32 + 32, :]] * 4
            sides.append(jnp.concatenate(pieces, axis=0))
        rhs = jnp.concatenate(sides, axis=1)
        left, columns = [], []
        for i in range(4):
            c = scal[16 + s, i]
            half_row, k = lax.div(c, 16), lax.rem(c, 16)
            quad, c4 = lax.div(k, 4), lax.rem(k, 4)
            rows = pl.ds(pl.multiple_of(quad * 128, 128), 128)
            t = panel[half_row, rows, :]
            t = jnp.concatenate([t[0:64], t[64:128]], axis=1)
            left.append(t * (quarter == c4).astype(F32).astype(BF16))
            columns.append(lax.rem(scal[half_row, k], 16))
        out = jnp.dot(jnp.concatenate(left, axis=0), rhs, preferred_element_type=F32)
        for i in range(4):
            h = i // 2
            got = out[i * 64 : i * 64 + 64, h * 128 : h * 128 + 128]
            got = jnp.where(half if i % 2 == 0 else jnp.logical_not(half), got, 0.0)
            out32[h, pl.ds(pl.multiple_of(columns[i] * 64, 64), 64), :] += got
        return carry

    lax.fori_loop(0, 16, step, 0, unroll=4)
    for h in range(2):
        for quad in range(4):
            for p in range(2):
                for c4 in range(4):
                    take = out32[h, pl.ds((quad * 4 + c4) * 64 + p, 32, stride=2), :]
                    at = quad * 256 + p * 128 + c4 * 32
                    (out_a, out_b)[h][at : at + 32, :] = take.astype(BF16)


def square_of(where, ring, other, slab):
    return pl.pallas_call(
        square_kernel,
        out_shape=(
            jax.ShapeDtypeStruct((2, 1024, 128), F32),
            *[jax.ShapeDtypeStruct((1024, 128), BF16)] * 2,
        ),
        in_specs=[SMEM] + [ANY] * 9,
        out_specs=(VMEM,) * 3,
        scratch_shapes=[
            pltpu.VMEM((16, HALF, 128), BF16),
            pltpu.VMEM((16, SLABP, 128), BF16),
            pltpu.VMEM((32, 128), I32),
            pltpu.SMEM((32, 128), I32),
            pltpu.SemaphoreType.DMA((9,)),
        ],
        compiler_params=PARAMS,
        name="square",
    )(where, *ring, *other, slab)


def cube_kernel(place_ref, *refs):
    ring, other, squares, outs = refs[:4], refs[4:8], refs[8:12], refs[12:16]
    panel, sq, acc, ints, scal, sem = refs[16:]
    x, y = place_ref[2], place_ref[3]
    copies = fetch_rows(place_ref, ring, other, panel, sem)
    more = []
    for n, part in enumerate(squares):
        more.append(pltpu.make_async_copy(part, sq.at[x ^ FLIPS[n]], sem.at[8 + n]))
    for copy in more:
        copy.start()
    acc[...] = jnp.zeros_like(acc)
    for copy in copies:
        copy.wait()
    read_columns(panel, ints)
    to_scal = pltpu.make_async_copy(ints, scal, sem.at[0])
    to_scal.start()
    to_scal.wait()
    for copy in more:
        copy.wait()
    quarter = lane_masks()
    masks = [(quarter == n).astype(F32).astype(BF16) for n in range(4)]

    def step(n, carry):
        source, quad = lax.div(n, 4), lax.rem(n, 4)
        right = sq[source, pl.ds(pl.multiple_of(quad * 256, 256), 256), :]
        rows = pl.ds(pl.multiple_of(quad * 128, 128), 128)
        for there in range(4):
            half_row = 8 * lax.rem(source, 2) + 2 * there + lax.div(source, 2)
            t = panel[half_row, rows, :]
            t = jnp.concatenate([t[0:64], t[64:128]], axis=1)
            left = jnp.concatenate([t * mask for mask in masks], axis=0)
            out = jnp.dot(left, right, preferred_element_type=F32)
            for c4 in range(4):
                j = lax.rem(scal[half_row, quad * 4 + c4], 16)
                into = pl.ds(pl.multiple_of(j * 64, 64), 64)
                acc[there, into, :] += out[c4 * 64 : c4 * 64 + 64, :]
        return carry

    lax.fori_loop(0, 16, step, 0, unroll=4)
    for n, out in enumerate(outs):
        out[...] = acc[y ^ FLIPS[n]].astype(out.dtype)


def cube_of(where, ring, other, squares):
    return pl.pallas_call(
        cube_kernel,
        out_shape=(
            jax.ShapeDtypeStruct((1024, 128), F32),
            *[jax.ShapeDtypeStruct((1024, 128), BF16)] * 3,
        ),
        in_specs=[SMEM] + [ANY] * 12,
        out_specs=(VMEM,) * 4,
        scratch_shapes=[
            pltpu.VMEM((16, HALF, 128), BF16),
            pltpu.VMEM((4, 1024, 128), BF16),
            pltpu.VMEM((4, 1024, 128), F32),
            pltpu.VMEM((16, 128), I32),
            pltpu.SMEM((16, 128), I32),
            pltpu.SemaphoreType.DMA((12,)),
        ],
        compiler_params=PARAMS,
        name="cube",
    )(where, *ring, *other, *squares)


def finish_kernel(sq_ref, *refs):
    out_ref = refs[8]
    for m in range(8):
        at = pl.ds(m * 128, 128)
        for h in range(2):
            cube = refs[4 * h][at, :]
            for ref in refs[4 * h + 1 : 4 * h + 4]:
                cube += ref[at, :].astype(F32)
            total = 3.0 * sq_ref[h, at, :] - 2.0 * cube
            out_ref[h * 128 : h * 128 + 128, at] = jnp.transpose(total)


def finish(square32, cubes):
    return pl.pallas_call(
        finish_kernel,
        out_shape=jax.ShapeDtypeStruct((256, 1024), F32),
        in_specs=[VMEM] * 9,
        out_specs=VMEM,
        compiler_params=PARAMS,
        name="finish",
    )(square32, *cubes)


def body(blocks, pattern):
    row, col, depth = (lax.axis_index(a) for a in AXES)
    where = jnp.stack([row // 2, row % 2, depth * 2 + col // 4, col % 4]).astype(I32)
    packed, slab = pack(blocks.reshape(32, 4096), pattern.reshape(1, 32))
    ring = ring_parts(packed)
    other = [swap(v, core=1) for v in ring]
    slab = lax.all_to_all(slab, ("col", "depth"), 0, 0, tiled=True)
    turned_ring = ring_parts(rows_to_y(packed))
    turned_other = None
    square32, *squares = square_of(where, ring, other, slab)
    cubes, moved = [], [()] * 3
    for mine in squares:
        moved = [swap(after(mine, *first), x=d) for d, first in zip(FLIPS[1:], moved)]
        if turned_other is None:
            turned_other = [swap(after(v, moved[0]), core=1) for v in turned_ring]
        own, *outs = cube_of(where, turned_ring, turned_other, [mine, *moved])
        moved = [(v,) for v in moved]
        outs = [swap(v, y=d) for v, d in zip(outs, FLIPS[1:])]
        cubes += [own, *outs]
    return finish(square32, cubes)


def solution(mesh):
    in_specs = (P("row", ("col", "depth"), None), P("row", ("col", "depth")))
    out_specs = P("row", ("col", "depth"))
    return jax.shard_map(body, mesh=mesh, in_specs=in_specs, out_specs=out_specs, check_vma=False)
```

```python
import functools

import jax
import jax.numpy as jnp
from jax import lax
from jax.experimental import pallas as pl
from jax.experimental.pallas import tpu as pltpu
from jax.sharding import PartitionSpec as P

AXES = ("row", "col", "depth")
F32, BF16, I32 = jnp.float32, jnp.bfloat16, jnp.int32
HALF = 528
SLABP = 144
VMEM_LIMIT = 40 << 20
PARAMS = pltpu.CompilerParams(vmem_limit_bytes=VMEM_LIMIT)


def place(i):
    row, col, depth = i // 16, i // 2 % 8, i % 2
    return row // 2, row % 2, depth * 2 + col // 4, col % 4


def index(z, core, x, y):
    return (z * 2 + core) * 16 + (x % 2 * 4 + y) * 2 + x // 2


def permute(value, target):
    pairs = [(i, index(*target(*place(i)))) for i in range(128)]
    return lax.ppermute(value, AXES, pairs)


def swap(value, z=0, core=0, x=0, y=0):
    return permute(value, lambda a, b, c, d: (a ^ z, b ^ core, c ^ x, d ^ y))


def after(value, *first):
    return lax.optimization_barrier((value, *first))[0]


def rows_to_y(value):
    def target(z, core, x, y):
        t = z % 2 * 2 + core
        return z // 2 * 2 + y // 2, y % 2, x, t

    return permute(value, target)


FLIPS = (0, 1, 3, 2)


def ring_parts(value):
    return [value] + [swap(value, z=d) for d in FLIPS[1:]]


def fetch_rows(place_ref, ring, other, panel, sem):
    z, core = place_ref[0], place_ref[1]
    copies = []
    for n in range(4):
        row = (z ^ FLIPS[n]) * 2
        mine, others = panel.at[pl.ds((row + core) * 2, 2)], panel.at[pl.ds((row + 1 - core) * 2, 2)]
        copies.append(pltpu.make_async_copy(ring[n], mine, sem.at[n]))
        copies.append(pltpu.make_async_copy(other[n], others, sem.at[4 + n]))
    for copy in copies:
        copy.start()
    return copies


def pack_kernel(x_hbm, pat_hbm, packed_ref, slab_ref, x_ref, pat_ref, rows, nat, turned, ints, sem):
    copies = [
        pltpu.make_async_copy(x_hbm, x_ref, sem.at[0]),
        pltpu.make_async_copy(pat_hbm, pat_ref, sem.at[1]),
    ]
    for copy in copies:
        copy.start()
    for copy in copies:
        copy.wait()
    for e in range(32):
        rows[pl.ds(e, 32, stride=32), :] = x_ref[:, e * 128 : e * 128 + 128].astype(F32)
    ints[...] = jnp.zeros_like(ints)
    for half in range(2):
        for quad in range(4):
            at = pl.ds(half * 512 + quad * 128, 128)
            packed_ref[half, quad * 128 : quad * 128 + 128, :] = jnp.transpose(rows[at, :]).astype(BF16)
        ints[0:1, 0:16] = pat_ref[0:1, half * 16 : half * 16 + 16]
        packed_ref[half, 512:528, :] = ints[...].astype(F32).astype(BF16)
    columns = packed_ref[0, 512:528, :]
    for i in range(4):
        part = rows[i * 32 : i * 32 + 32, :]
        nat[pl.ds(i * 64, 32, stride=2), :] = part
        nat[pl.ds(i * 64 + 1, 32, stride=2), :] = pltpu.roll(part, 64, 1)
    for h in range(2):
        turned[...] = jnp.transpose(nat[h * 128 : h * 128 + 128, :])
        for p in range(2):
            piece = turned[pl.ds(p, 32, stride=2), :].astype(BF16)
            at = h * 64 + p * 32
            for s in range(16):
                slab_ref[s, at : at + 32, :] = piece
    for s in range(16):
        slab_ref[s, 128:144, :] = columns


ANY = pl.BlockSpec(memory_space=pl.ANY)
HBM = pl.BlockSpec(memory_space=pltpu.HBM)
SMEM = pl.BlockSpec(memory_space=pltpu.SMEM)
VMEM = pl.BlockSpec(memory_space=pltpu.VMEM)


def pack(blocks, pattern):
    return pl.pallas_call(
        pack_kernel,
        out_shape=(
            jax.ShapeDtypeStruct((2, HALF, 128), BF16),
            jax.ShapeDtypeStruct((16, SLABP, 128), BF16),
        ),
        in_specs=[HBM, HBM],
        out_specs=(VMEM, VMEM),
        scratch_shapes=[
            pltpu.VMEM((32, 4096), BF16),
            pltpu.VMEM((1, 32), I32),
            pltpu.VMEM((1024, 128), F32),
            pltpu.VMEM((256, 128), F32),
            pltpu.VMEM((128, 128), F32),
            pltpu.VMEM((16, 128), I32),
            pltpu.SemaphoreType.DMA((2,)),
        ],
        compiler_params=pltpu.CompilerParams(vmem_limit_bytes=62 << 20),
        name="pack",
    )(blocks, pattern)


def read_columns(panel, ints):
    for n in range(16):
        row = panel[n, 512:528, :].astype(F32)[0:1, :]
        ints[n : n + 1, :] = row.astype(I32)


def lane_masks():
    lane = lax.broadcasted_iota(I32, (1, 256), 1)
    return lax.rem(lax.div(lane, 32), 4)


def square_kernel(place_ref, *refs):
    ring, other, slab_ref = refs[:4], refs[4:8], refs[8]
    out32, out_a, out_b, panel, slab, ints, scal, sem = refs[9:]
    copies = fetch_rows(place_ref, ring, other, panel, sem)
    fetch_slab = pltpu.make_async_copy(slab_ref, slab, sem.at[8])
    fetch_slab.start()
    out32[...] = jnp.zeros_like(out32)
    fetch_slab.wait()
    for s in range(16):
        ints[16 + s : 17 + s, :] = slab[s, 128:144, :].astype(F32)[0:1, :].astype(I32)
    for copy in copies:
        copy.wait()
    read_columns(panel, ints)
    to_scal = pltpu.make_async_copy(ints, scal, sem.at[0])
    to_scal.start()
    to_scal.wait()
    quarter = lane_masks()
    half = lax.broadcasted_iota(I32, (64, 128), 1) < 64

    def step(s, carry):
        sides = []
        for h in range(2):
            pieces = []
            for p in range(2):
                pieces += [slab[s, h * 64 + p * 32 : h * 64 + p * 32 + 32, :]] * 4
            sides.append(jnp.concatenate(pieces, axis=0))
        rhs = jnp.concatenate(sides, axis=1)
        left, columns = [], []
        for i in range(4):
            c = scal[16 + s, i]
            half_row, k = lax.div(c, 16), lax.rem(c, 16)
            quad, c4 = lax.div(k, 4), lax.rem(k, 4)
            rows = pl.ds(pl.multiple_of(quad * 128, 128), 128)
            t = panel[half_row, rows, :]
            t = jnp.concatenate([t[0:64], t[64:128]], axis=1)
            left.append(t * (quarter == c4).astype(F32).astype(BF16))
            columns.append(lax.rem(scal[half_row, k], 16))
        out = jnp.dot(jnp.concatenate(left, axis=0), rhs, preferred_element_type=F32)
        for i in range(4):
            h = i // 2
            got = out[i * 64 : i * 64 + 64, h * 128 : h * 128 + 128]
            got = jnp.where(half if i % 2 == 0 else jnp.logical_not(half), got, 0.0)
            out32[h, pl.ds(pl.multiple_of(columns[i] * 64, 64), 64), :] += got
        return carry

    lax.fori_loop(0, 16, step, 0, unroll=4)
    for h in range(2):
        for quad in range(4):
            for p in range(2):
                for c4 in range(4):
                    take = out32[h, pl.ds((quad * 4 + c4) * 64 + p, 32, stride=2), :]
                    at = quad * 256 + p * 128 + c4 * 32
                    (out_a, out_b)[h][at : at + 32, :] = take.astype(BF16)


def square_of(where, ring, other, slab):
    return pl.pallas_call(
        square_kernel,
        out_shape=(
            jax.ShapeDtypeStruct((2, 1024, 128), F32),
            *[jax.ShapeDtypeStruct((1024, 128), BF16)] * 2,
        ),
        in_specs=[SMEM] + [ANY] * 9,
        out_specs=(VMEM,) * 3,
        scratch_shapes=[
            pltpu.VMEM((16, HALF, 128), BF16),
            pltpu.VMEM((16, SLABP, 128), BF16),
            pltpu.VMEM((32, 128), I32),
            pltpu.SMEM((32, 128), I32),
            pltpu.SemaphoreType.DMA((9,)),
        ],
        compiler_params=PARAMS,
        name="square",
    )(where, *ring, *other, slab)


def columns_kernel(same, other, scal, ints, sem):
    for b, ref in enumerate((same, other)):
        for n in range(8):
            row = ref[n // 2, n % 2, 512:528, :].astype(F32)[0:1, :]
            ints[8 * b + n : 8 * b + n + 1, :] = row.astype(I32)
    to_scal = pltpu.make_async_copy(ints, scal, sem)
    to_scal.start()
    to_scal.wait()


def columns_of(same, other):
    return pl.pallas_call(
        columns_kernel,
        out_shape=jax.ShapeDtypeStruct((16, 128), I32),
        in_specs=[VMEM, VMEM],
        out_specs=SMEM,
        scratch_shapes=[pltpu.VMEM((16, 128), I32), pltpu.SemaphoreType.DMA],
        compiler_params=PARAMS,
        name="columns",
    )(same, other)


def cube_kernel(place_ref, scal, same, other, *refs):
    squares, outs, (acc,) = refs[:4], refs[4:8], refs[8:]
    z, core, x, y = (place_ref[n] for n in range(4))
    acc[...] = jnp.zeros_like(acc)
    quarter = lane_masks()
    masks = [(quarter == n).astype(F32).astype(BF16) for n in range(4)]

    for n in range(4):
        source = x ^ FLIPS[n]
        half = lax.div(source, 2)

        def step(quad, carry, n=n, source=source, half=half):
            right = squares[n][pl.ds(pl.multiple_of(quad * 256, 256), 256), :]
            rows = pl.ds(pl.multiple_of(quad * 128, 128), 128)
            for b, panel in enumerate((same, other)):
                for m in range(2):
                    there = 2 * m + (core ^ b)
                    flip = z ^ (2 * lax.rem(source, 2) + m)
                    at = flip ^ lax.div(flip, 2)
                    t = panel[at, half, rows, :]
                    t = jnp.concatenate([t[0:64], t[64:128]], axis=1)
                    left = jnp.concatenate([t * mask for mask in masks], axis=0)
                    out = jnp.dot(left, right, preferred_element_type=F32)
                    for c4 in range(4):
                        j = lax.rem(scal[8 * b + 2 * at + half, quad * 4 + c4], 16)
                        into = pl.ds(pl.multiple_of(j * 64, 64), 64)
                        acc[there, into, :] += out[c4 * 64 : c4 * 64 + 64, :]
            return carry

        lax.fori_loop(0, 4, step, 0, unroll=True)
    for n, out in enumerate(outs):
        out[...] = acc[y ^ FLIPS[n]].astype(out.dtype)


def cube_of(where, columns, same, other, squares):
    return pl.pallas_call(
        cube_kernel,
        out_shape=(
            jax.ShapeDtypeStruct((1024, 128), F32),
            *[jax.ShapeDtypeStruct((1024, 128), BF16)] * 3,
        ),
        in_specs=[SMEM, SMEM] + [VMEM] * 6,
        out_specs=(VMEM,) * 4,
        scratch_shapes=[pltpu.VMEM((4, 1024, 128), F32)],
        compiler_params=PARAMS,
        name="cube",
    )(where, columns, same, other, *squares)


def finish_kernel(h, sq_ref, own_ref, a_ref, b_ref, c_ref, *refs):
    out_ref = refs[-1]
    for m in range(8):
        at = pl.ds(m * 128, 128)
        cube = own_ref[at, :]
        for ref in (a_ref, b_ref, c_ref):
            cube += ref[at, :].astype(F32)
        out_ref[:, at] = jnp.transpose(3.0 * sq_ref[h, at, :] - 2.0 * cube)


def finish(h, square32, cubes, before):
    return pl.pallas_call(
        functools.partial(finish_kernel, h),
        out_shape=jax.ShapeDtypeStruct((256, 1024), F32),
        grid=(1,),
        in_specs=[VMEM] * 5 + [ANY] * len(before),
        out_specs=pl.BlockSpec((128, 1024), lambda i: (h, 0)),
        input_output_aliases={5: 0} if before else {},
        compiler_params=PARAMS,
        name="finish",
    )(square32, *cubes, *before)


def body(blocks, pattern):
    row, col, depth = (lax.axis_index(a) for a in AXES)
    where = jnp.stack([row // 2, row % 2, depth * 2 + col // 4, col % 4]).astype(I32)
    packed, slab = pack(blocks.reshape(32, 4096), pattern.reshape(1, 32))
    ring = ring_parts(packed)
    other = [swap(v, core=1) for v in ring]
    slab = lax.all_to_all(slab, ("col", "depth"), 0, 0, tiled=True)
    turned_ring = ring_parts(rows_to_y(packed))
    turned_other = None
    square32, *squares = square_of(where, ring, other, slab)
    cubes, moved = [], [()] * 3
    for mine in squares:
        moved = [swap(after(mine, *first), x=d) for d, first in zip(FLIPS[1:], moved)]
        if turned_other is None:
            turned = jnp.stack(turned_ring)
            turned_other = swap(after(turned, *moved), core=1)
            columns = columns_of(turned, turned_other)
        own, *outs = cube_of(where, columns, turned, turned_other, [mine, *moved])
        moved = [(v,) for v in moved]
        outs = [swap(v, y=d) for v, d in zip(outs, FLIPS[1:])]
        cubes.append([own, *outs])
    first = finish(0, square32, cubes[0], [])
    return finish(1, square32, cubes[1], [first])


def solution(mesh):
    in_specs = (P("row", ("col", "depth"), None), P("row", ("col", "depth")))
    out_specs = P("row", ("col", "depth"))
    return jax.shard_map(body, mesh=mesh, in_specs=in_specs, out_specs=out_specs, check_vma=False)
```

```python
import functools

import jax
import jax.numpy as jnp
from jax import lax
from jax.experimental import pallas as pl
from jax.experimental.pallas import tpu as pltpu
from jax.sharding import PartitionSpec as P

AXES = ("row", "col", "depth")
F32, BF16, I32 = jnp.float32, jnp.bfloat16, jnp.int32
HALF = 528
SLABP = 144
VMEM_LIMIT = 40 << 20
PARAMS = pltpu.CompilerParams(vmem_limit_bytes=VMEM_LIMIT)


def place(i):
    row, col, depth = i // 16, i // 2 % 8, i % 2
    return row // 2, row % 2, depth * 2 + col // 4, col % 4


def index(z, core, x, y):
    return (z * 2 + core) * 16 + (x % 2 * 4 + y) * 2 + x // 2


def permute(value, target):
    pairs = [(i, index(*target(*place(i)))) for i in range(128)]
    return lax.ppermute(value, AXES, pairs)


def swap(value, z=0, core=0, x=0, y=0):
    return permute(value, lambda a, b, c, d: (a ^ z, b ^ core, c ^ x, d ^ y))


def after(value, *first):
    return lax.optimization_barrier((value, *first))[0]


def rows_to_y(value):
    def target(z, core, x, y):
        t = z % 2 * 2 + core
        return z // 2 * 2 + y // 2, y % 2, x, t

    return permute(value, target)


FLIPS = (0, 1, 3, 2)


def ring_parts(value):
    return [value] + [swap(value, z=d) for d in FLIPS[1:]]


def fetch_rows(place_ref, ring, other, panel, sem):
    z, core = place_ref[0], place_ref[1]
    copies = []
    for n in range(4):
        row = (z ^ FLIPS[n]) * 2
        mine, others = panel.at[pl.ds((row + core) * 2, 2)], panel.at[pl.ds((row + 1 - core) * 2, 2)]
        copies.append(pltpu.make_async_copy(ring[n], mine, sem.at[n]))
        copies.append(pltpu.make_async_copy(other[n], others, sem.at[4 + n]))
    for copy in copies:
        copy.start()
    return copies


def pack_kernel(x_hbm, pat_hbm, packed_ref, slab_ref, x_ref, pat_ref, rows, nat, turned, ints, sem):
    copies = [
        pltpu.make_async_copy(x_hbm, x_ref, sem.at[0]),
        pltpu.make_async_copy(pat_hbm, pat_ref, sem.at[1]),
    ]
    for copy in copies:
        copy.start()
    for copy in copies:
        copy.wait()
    for e in range(32):
        rows[pl.ds(e, 32, stride=32), :] = x_ref[:, e * 128 : e * 128 + 128].astype(F32)
    ints[...] = jnp.zeros_like(ints)
    for half in range(2):
        for quad in range(4):
            at = pl.ds(half * 512 + quad * 128, 128)
            packed_ref[half, quad * 128 : quad * 128 + 128, :] = jnp.transpose(rows[at, :]).astype(BF16)
        ints[0:1, 0:16] = pat_ref[0:1, half * 16 : half * 16 + 16]
        packed_ref[half, 512:528, :] = ints[...].astype(F32).astype(BF16)
    columns = packed_ref[0, 512:528, :]
    for i in range(4):
        part = rows[i * 32 : i * 32 + 32, :]
        nat[pl.ds(i * 64, 32, stride=2), :] = part
        nat[pl.ds(i * 64 + 1, 32, stride=2), :] = pltpu.roll(part, 64, 1)
    for h in range(2):
        turned[...] = jnp.transpose(nat[h * 128 : h * 128 + 128, :])
        for p in range(2):
            piece = turned[pl.ds(p, 32, stride=2), :].astype(BF16)
            at = h * 64 + p * 32
            for s in range(16):
                slab_ref[s, at : at + 32, :] = piece
    for s in range(16):
        slab_ref[s, 128:144, :] = columns


ANY = pl.BlockSpec(memory_space=pl.ANY)
HBM = pl.BlockSpec(memory_space=pltpu.HBM)
SMEM = pl.BlockSpec(memory_space=pltpu.SMEM)
VMEM = pl.BlockSpec(memory_space=pltpu.VMEM)


def pack(blocks, pattern):
    return pl.pallas_call(
        pack_kernel,
        out_shape=(
            jax.ShapeDtypeStruct((2, HALF, 128), BF16),
            jax.ShapeDtypeStruct((16, SLABP, 128), BF16),
        ),
        in_specs=[HBM, HBM],
        out_specs=(VMEM, VMEM),
        scratch_shapes=[
            pltpu.VMEM((32, 4096), BF16),
            pltpu.VMEM((1, 32), I32),
            pltpu.VMEM((1024, 128), F32),
            pltpu.VMEM((256, 128), F32),
            pltpu.VMEM((128, 128), F32),
            pltpu.VMEM((16, 128), I32),
            pltpu.SemaphoreType.DMA((2,)),
        ],
        compiler_params=pltpu.CompilerParams(vmem_limit_bytes=62 << 20),
        name="pack",
    )(blocks, pattern)


def read_columns(panel, ints):
    for n in range(16):
        row = panel[n, 512:528, :].astype(F32)[0:1, :]
        ints[n : n + 1, :] = row.astype(I32)


def lane_masks():
    lane = lax.broadcasted_iota(I32, (1, 256), 1)
    return lax.rem(lax.div(lane, 32), 4)


def square_kernel(place_ref, *refs):
    ring, other, slab_ref = refs[:4], refs[4:8], refs[8]
    out32, out_a, out_b, panel, slab, ints, scal, sem = refs[9:]
    copies = fetch_rows(place_ref, ring, other, panel, sem)
    fetch_slab = pltpu.make_async_copy(slab_ref, slab, sem.at[8])
    fetch_slab.start()
    out32[...] = jnp.zeros_like(out32)
    fetch_slab.wait()
    for s in range(16):
        ints[16 + s : 17 + s, :] = slab[s, 128:144, :].astype(F32)[0:1, :].astype(I32)
    for copy in copies:
        copy.wait()
    read_columns(panel, ints)
    to_scal = pltpu.make_async_copy(ints, scal, sem.at[0])
    to_scal.start()
    to_scal.wait()
    quarter = lane_masks()
    half = lax.broadcasted_iota(I32, (64, 128), 1) < 64

    def step(s, carry):
        sides = []
        for h in range(2):
            pieces = []
            for p in range(2):
                pieces += [slab[s, h * 64 + p * 32 : h * 64 + p * 32 + 32, :]] * 4
            sides.append(jnp.concatenate(pieces, axis=0))
        rhs = jnp.concatenate(sides, axis=1)
        left, columns = [], []
        for i in range(4):
            c = scal[16 + s, i]
            half_row, k = lax.div(c, 16), lax.rem(c, 16)
            quad, c4 = lax.div(k, 4), lax.rem(k, 4)
            rows = pl.ds(pl.multiple_of(quad * 128, 128), 128)
            t = panel[half_row, rows, :]
            t = jnp.concatenate([t[0:64], t[64:128]], axis=1)
            left.append(t * (quarter == c4).astype(F32).astype(BF16))
            columns.append(lax.rem(scal[half_row, k], 16))
        out = jnp.dot(jnp.concatenate(left, axis=0), rhs, preferred_element_type=F32)
        for i in range(4):
            h = i // 2
            got = out[i * 64 : i * 64 + 64, h * 128 : h * 128 + 128]
            got = jnp.where(half if i % 2 == 0 else jnp.logical_not(half), got, 0.0)
            out32[h, pl.ds(pl.multiple_of(columns[i] * 64, 64), 64), :] += got
        return carry

    lax.fori_loop(0, 16, step, 0, unroll=4)
    for h in range(2):
        for quad in range(4):
            for p in range(2):
                for c4 in range(4):
                    take = out32[h, pl.ds((quad * 4 + c4) * 64 + p, 32, stride=2), :]
                    at = quad * 256 + p * 128 + c4 * 32
                    (out_a, out_b)[h][at : at + 32, :] = take.astype(BF16)


def square_of(where, ring, other, slab):
    return pl.pallas_call(
        square_kernel,
        out_shape=(
            jax.ShapeDtypeStruct((2, 1024, 128), F32),
            *[jax.ShapeDtypeStruct((1024, 128), BF16)] * 2,
        ),
        in_specs=[SMEM] + [ANY] * 9,
        out_specs=(VMEM,) * 3,
        scratch_shapes=[
            pltpu.VMEM((16, HALF, 128), BF16),
            pltpu.VMEM((16, SLABP, 128), BF16),
            pltpu.VMEM((32, 128), I32),
            pltpu.SMEM((32, 128), I32),
            pltpu.SemaphoreType.DMA((9,)),
        ],
        compiler_params=PARAMS,
        name="square",
    )(where, *ring, *other, slab)


def columns_kernel(part, scal, ints, sem):
    for n in range(8):
        row = part[n // 2, n % 2, 512:528, :].astype(F32)[0:1, :]
        ints[n : n + 1, :] = row.astype(I32)
    to_scal = pltpu.make_async_copy(ints, scal, sem)
    to_scal.start()
    to_scal.wait()


def columns_of(part):
    return pl.pallas_call(
        columns_kernel,
        out_shape=jax.ShapeDtypeStruct((8, 128), I32),
        in_specs=[VMEM],
        out_specs=SMEM,
        scratch_shapes=[pltpu.VMEM((8, 128), I32), pltpu.SemaphoreType.DMA],
        compiler_params=PARAMS,
        name="columns",
    )(part)


def cube_kernel(place_ref, scal_same, scal_other, same, other, *refs):
    squares, outs, (acc,) = refs[:4], refs[4:8], refs[8:]
    z, core, x, y = (place_ref[n] for n in range(4))
    acc[...] = jnp.zeros_like(acc)
    quarter = lane_masks()
    masks = [(quarter == n).astype(F32).astype(BF16) for n in range(4)]

    for n in range(4):
        source = x ^ FLIPS[n]
        half = lax.div(source, 2)

        def step(quad, carry, n=n, source=source, half=half):
            right = squares[n][pl.ds(pl.multiple_of(quad * 256, 256), 256), :]
            rows = pl.ds(pl.multiple_of(quad * 128, 128), 128)
            for b, (panel, scal) in enumerate(((same, scal_same), (other, scal_other))):
                for m in range(2):
                    there = 2 * m + (core ^ b)
                    flip = z ^ (2 * lax.rem(source, 2) + m)
                    at = flip ^ lax.div(flip, 2)
                    t = panel[at, half, rows, :]
                    t = jnp.concatenate([t[0:64], t[64:128]], axis=1)
                    left = jnp.concatenate([t * mask for mask in masks], axis=0)
                    out = jnp.dot(left, right, preferred_element_type=F32)
                    for c4 in range(4):
                        j = lax.rem(scal[2 * at + half, quad * 4 + c4], 16)
                        into = pl.ds(pl.multiple_of(j * 64, 64), 64)
                        acc[there, into, :] += out[c4 * 64 : c4 * 64 + 64, :]
            return carry

        lax.fori_loop(0, 4, step, 0, unroll=True)
    for n, out in enumerate(outs):
        out[...] = acc[y ^ FLIPS[n]].astype(out.dtype)


def cube_of(where, columns, same, other, squares):
    return pl.pallas_call(
        cube_kernel,
        out_shape=(
            jax.ShapeDtypeStruct((1024, 128), F32),
            *[jax.ShapeDtypeStruct((1024, 128), BF16)] * 3,
        ),
        in_specs=[SMEM] * 3 + [VMEM] * 6,
        out_specs=(VMEM,) * 4,
        scratch_shapes=[pltpu.VMEM((4, 1024, 128), F32)],
        compiler_params=PARAMS,
        name="cube",
    )(where, *columns, same, other, *squares)


def finish_kernel(h, sq_ref, own_ref, a_ref, b_ref, c_ref, *refs):
    out_ref = refs[-1]
    for m in range(8):
        at = pl.ds(m * 128, 128)
        cube = own_ref[at, :]
        for ref in (a_ref, b_ref, c_ref):
            cube += ref[at, :].astype(F32)
        out_ref[:, at] = jnp.transpose(3.0 * sq_ref[h, at, :] - 2.0 * cube)


def finish(h, square32, cubes, before):
    return pl.pallas_call(
        functools.partial(finish_kernel, h),
        out_shape=jax.ShapeDtypeStruct((256, 1024), F32),
        grid=(1,),
        in_specs=[VMEM] * 5 + [ANY] * len(before),
        out_specs=pl.BlockSpec((128, 1024), lambda i: (h, 0)),
        input_output_aliases={5: 0} if before else {},
        compiler_params=PARAMS,
        name="finish",
    )(square32, *cubes, *before)


def body(blocks, pattern):
    row, col, depth = (lax.axis_index(a) for a in AXES)
    where = jnp.stack([row // 2, row % 2, depth * 2 + col // 4, col % 4]).astype(I32)
    packed, slab = pack(blocks.reshape(32, 4096), pattern.reshape(1, 32))
    ring = ring_parts(packed)
    other = [swap(v, core=1) for v in ring]
    slab = lax.all_to_all(slab, ("col", "depth"), 0, 0, tiled=True)
    turned_ring = ring_parts(rows_to_y(packed))
    turned_other = None
    square32, *squares = square_of(where, ring, other, slab)
    cubes, moved = [], [()] * 3
    for mine in squares:
        moved = [swap(after(mine, *first), x=d) for d, first in zip(FLIPS[1:], moved)]
        if turned_other is None:
            turned = jnp.stack(turned_ring)
            turned_other = swap(after(turned, *moved), core=1)
            columns = [columns_of(turned), columns_of(turned_other)]
        own, *outs = cube_of(where, columns, turned, turned_other, [mine, *moved])
        moved = [(v,) for v in moved]
        outs = [swap(v, y=d) for v, d in zip(outs, FLIPS[1:])]
        cubes.append([own, *outs])
    first = finish(0, square32, cubes[0], [])
    return finish(1, square32, cubes[1], [first])


def solution(mesh):
    in_specs = (P("row", ("col", "depth"), None), P("row", ("col", "depth")))
    out_specs = P("row", ("col", "depth"))
    return jax.shard_map(body, mesh=mesh, in_specs=in_specs, out_specs=out_specs, check_vma=False)
```
